32 devices in a mesh: member: 8 (over z, core), space: 4 (over y, x).
Axes of the slice: x: 2, y: 2, z: 4, core: 2. Of those that a mesh axis runs over, the one named last changes fastest.
Arguments:
- latents: bfloat16 [3072, 512], P('space'), may hold values from -6 to 6
- sample_perturbation: bfloat16 [24, 3072, 512], P('member', 'space'), may hold values from -6 to 6
- noise_table: float32 [64, 512], replicated, may hold values from 0.2 to 1.5
- member_seed: int32 [24], P('member'), may hold values from 0 to 63
- piece_arrangement: int32 [768], replicated, may hold values from 0 to 767, each once
- targets: bfloat16 [3072, 384], P('space'), may hold values from -4 to 4
- w_gate: bfloat16 [512, 1024], replicated, may hold values from -0.25 to 0.25
- w_up: bfloat16 [512, 1024], replicated, may hold values from -0.25 to 0.25
- lowering_matrix: bfloat16 [1024, 384], replicated, may hold values from -0.1875 to 0.1875
Outputs:
- latent_grad: float32 [3072, 512], P('space', 'member')
The draws below stay inside these ranges and needn't reach their ends.
Inputs may be any that keep to these rules, and one draw needn't show every extreme that they name: `piece_arrangement`: a permutation of the 768 positions of a tile, the same for every tile.
All inputs are finite; a program needn't handle non-finite values.
Results may differ from the reference program's by a relative error of at most 0.0019.
Values may be sent and summed in bfloat16 or wider, within the bound.
A program may use at most 128 MiB of HBM per device.

```python
import jax
import jax.numpy as jnp
from jax import lax

LAT = 512
HID = 1024
RESULT_DIM = 384
PIECE_ITEMS = 8
TABLE = 64
REGION_ITEMS = 768
MEMBERS = 24
TOKENS = 3072


def touch_ends(values, own_key, smallest, largest):
    shape = values.shape
    place = [jax.random.randint(jax.random.fold_in(own_key, axis), (), 0, shape[axis]) for axis in range(len(shape))]
    values = values.at[tuple(place)].set(smallest)
    longest = shape.index(max(shape))
    place[longest] = (place[longest] + 1) % shape[longest]
    return values.at[tuple(place)].set(largest)


def block_levels(rng, shape, shards, least, largest):
    loudness, own = 1.0, jax.random.fold_in(rng, 6)
    for axis_at, parts in shards:
        steps = jnp.exp(jax.random.uniform(jax.random.fold_in(own, axis_at), (parts,), jnp.float32, least / len(shards), largest / len(shards)))
        loudness = loudness * jnp.repeat(steps, shape[axis_at] // parts).reshape([-1 if axis == axis_at else 1 for axis in range(len(shape))])
    return loudness


def noise(stream_key, dims, deviation, reach, split=(), kind=jnp.bfloat16):
    level = block_levels(stream_key, dims, split, -0.22, 0.18) if split else 1.0
    values = jax.random.normal(stream_key, dims, jnp.float32) * deviation * level
    return jnp.minimum(jnp.maximum(values, -reach), reach).astype(kind)


def setup_inputs(seed: int = 0) -> dict:
    streams_of = jax.random.split(jax.random.key(seed), 10)
    return {
        "latents": noise(streams_of[0], (TOKENS, LAT), 1.0, 6.0, ((0, 4),)),
        "sample_perturbation": noise(streams_of[1], (MEMBERS, TOKENS, LAT), 1.0, 6.0, ((0, 8), (1, 4))),
        "noise_table": jnp.clip(jax.random.uniform(streams_of[2], (TABLE, LAT), jnp.float32, 0.2, 1.5), 0.2, 1.5),
        "member_seed": touch_ends(jax.random.randint(streams_of[3], (MEMBERS,), 0, TABLE), jax.random.fold_in(streams_of[3], 1), 0, TABLE - 1).astype(jnp.int32),
        "piece_arrangement": jax.random.permutation(streams_of[4], REGION_ITEMS).astype(jnp.int32),
        "targets": noise(streams_of[5], (TOKENS, RESULT_DIM), 0.5, 4.0, ((0, 4),)),
        "w_gate": noise(streams_of[6], (LAT, HID), LAT ** -0.5, 0.25),
        "w_up": noise(streams_of[7], (LAT, HID), LAT ** -0.5, 0.25),
        "lowering_matrix": noise(streams_of[8], (HID, RESULT_DIM), HID ** -0.5, 0.1875),
    }


def apply_network(noisy_input, w_gate, w_up, lowering_matrix):
    sigmoid_branch_signal = jnp.dot(noisy_input, w_gate, preferred_element_type=jnp.float32)
    raising_signal = jnp.dot(noisy_input, w_up, preferred_element_type=jnp.float32)
    inner_signal = (sigmoid_branch_signal * jax.nn.sigmoid(sigmoid_branch_signal) * raising_signal).astype(jnp.bfloat16)
    predicted_values = jnp.dot(inner_signal, lowering_matrix, preferred_element_type=jnp.float32).astype(jnp.bfloat16)
    return (sigmoid_branch_signal, raising_signal, predicted_values)

def run_backward(cotangent, sigmoid_branch_signal, raising_signal, w_gate, w_up, lowering_matrix):
    hidden_grad = jnp.dot(cotangent, lowering_matrix.T, preferred_element_type=jnp.float32)
    sigmoid_gate = jax.nn.sigmoid(sigmoid_branch_signal)
    gate_grad = (hidden_grad * raising_signal * sigmoid_gate * (1.0 + sigmoid_branch_signal * (1.0 - sigmoid_gate))).astype(jnp.bfloat16)
    up_grad = (hidden_grad * sigmoid_branch_signal * sigmoid_gate).astype(jnp.bfloat16)
    first = jnp.dot(gate_grad, w_gate.T, preferred_element_type=jnp.float32)
    return first + jnp.dot(up_grad, w_up.T, preferred_element_type=jnp.float32)

def scoring_rule(predicted_item_matrix, observed_item_matrix):
    sample_discrepancy = predicted_item_matrix - observed_item_matrix
    return sample_discrepancy / jnp.sqrt(lax.optimization_barrier(jnp.sum(sample_discrepancy * sample_discrepancy, axis=-1, keepdims=True)) + 1.0)

def spread_fn(members_block, loss_scale):
    count = members_block.shape[0]
    wide_block = members_block.astype(jnp.float32)
    gram_matrix = jnp.einsum('mkf,nkf->kmn', wide_block, wide_block)
    diagonal = jnp.diagonal(gram_matrix, axis1=1, axis2=2)
    squared_gap = diagonal[:, :, None] + diagonal[:, None, :] - 2.0 * gram_matrix
    identity_mask = jnp.eye(count, dtype=bool)[None]
    distance = jnp.sqrt(jnp.where(identity_mask, 0.0, squared_gap) + 1.0)
    pair_weight = (1.0 / distance).astype(jnp.bfloat16)
    wide_weight = pair_weight.astype(jnp.float32)
    row_total = lax.optimization_barrier(jnp.sum(wide_weight, axis=2))
    weighted = jnp.einsum('kmn,nkf->mkf', wide_weight, wide_block)
    spread = loss_scale / count * (row_total.T[:, :, None] * wide_block - weighted)
    return spread.astype(jnp.bfloat16)

def reference(latents, sample_perturbation, noise_table, member_seed, piece_arrangement, targets, w_gate, w_up, lowering_matrix):
    sample_sequence = sample_perturbation.shape[0]
    region_blocks = latents.shape[0] // REGION_ITEMS
    embedding_matrix = PIECE_ITEMS * RESULT_DIM
    loss_scale = float(embedding_matrix) ** 0.5
    one_hot = (member_seed[:, None] == jnp.arange(TABLE, dtype=jnp.int32)[None, :]).astype(jnp.float32)
    component_multiplier = jnp.dot(one_hot, noise_table, precision=lax.Precision.HIGHEST)
    latent_rows = latents.astype(jnp.float32)

    def noisy(member_rows, member_scale):
        return (latent_rows + member_rows.astype(jnp.float32) * member_scale[None, :]).astype(jnp.bfloat16)

    def evaluate_ensemble_sample(paired):
        return apply_network(noisy(paired[0], paired[1]), w_gate, w_up, lowering_matrix)[2]
    predicted_values = lax.map(evaluate_ensemble_sample, (sample_perturbation, component_multiplier))
    piece_item_matrix = predicted_values.reshape(sample_sequence, region_blocks, REGION_ITEMS, RESULT_DIM)[:, :, piece_arrangement].reshape(sample_sequence, region_blocks * (REGION_ITEMS // PIECE_ITEMS), embedding_matrix)
    observed_item_matrix = targets.reshape(region_blocks, REGION_ITEMS, RESULT_DIM)[:, piece_arrangement].reshape(region_blocks * (REGION_ITEMS // PIECE_ITEMS), embedding_matrix).astype(jnp.float32)
    skill_term = scoring_rule(piece_item_matrix.astype(jnp.float32), observed_item_matrix[None])
    spread = spread_fn(piece_item_matrix, loss_scale)
    cotangent = (loss_scale * skill_term - spread.astype(jnp.float32)).astype(jnp.bfloat16)
    inverse_order = jnp.argsort(piece_arrangement).astype(jnp.int32)
    cotangent = cotangent.reshape(sample_sequence, region_blocks, REGION_ITEMS, RESULT_DIM)[:, :, inverse_order].reshape(sample_sequence, region_blocks * REGION_ITEMS, RESULT_DIM)

    def accumulate(total, triple):
        sigmoid_branch_signal, raising_signal, ignored = apply_network(noisy(triple[0], triple[1]), w_gate, w_up, lowering_matrix)
        return (total + run_backward(triple[2], sigmoid_branch_signal, raising_signal, w_gate, w_up, lowering_matrix), None)
    total, ignored = lax.scan(accumulate, jnp.zeros(latents.shape, jnp.float32), (sample_perturbation, component_multiplier, cotangent))
    return total
```

```python
import functools

import jax
import jax.numpy as jnp
from jax import lax
from jax.experimental import pallas as pl
from jax.experimental.pallas import tpu as pltpu
from jax.sharding import PartitionSpec as P

PIECE_ITEMS = 8
ROWS = 16
LANES = 128
F32 = jnp.float32
BF16 = jnp.bfloat16


def dot(a, b, last=False):
    dims = (((1,), (1,)), ((), ())) if last else (((1,), (0,)), ((), ()))
    return lax.dot_general(a, b, dims, preferred_element_type=F32)


def three_way(x):
    high = x.astype(BF16)
    rest = x - high.astype(F32)
    mid = rest.astype(BF16)
    return high, mid, (rest - mid.astype(F32)).astype(BF16)


def kernel(
    n, own, chunks, block, hid_tile,
    seed_ref, lat_ref, pert_ref, table_ref, arr_row_ref, arr_col_ref,
    tgt_hbm, wg_hbm, wu_hbm, low_hbm,
    out_ref,
    tgt_ref, wg_ref, wu_ref, low_ref,
    order, order_t, noisy, target, send, recv, hidden, gate_factor, up_factor, forecast, cotangent,
    grads, back_send, back_recv,
    load_sem, send_sem, recv_sem, back_send_sem, back_recv_sem,
):
    me = lax.axis_index("member")
    tokens, width = lat_ref.shape
    members = n * own
    hid = wg_ref.shape[1]
    result = low_ref.shape[1]
    scale = float(PIECE_ITEMS * result) ** 0.5
    far_first = sorted(range(1, n), key=lambda k: abs(k - n // 2))

    barrier = pltpu.get_barrier_semaphore()
    for k in range(1, n):
        pl.semaphore_signal(
            barrier, inc=1, device_id={"member": lax.rem(me + k, n)},
            device_id_type=pl.DeviceIdType.MESH,
        )
    loads = [
        pltpu.make_async_copy(src, dst, load_sem.at[i])
        for i, (src, dst) in enumerate(
            ((tgt_hbm, tgt_ref), (wg_hbm, wg_ref), (wu_hbm, wu_ref), (low_hbm, low_ref))
        )
    ]
    for load in loads:
        load.start()

    def piece(c, d, s):
        return pltpu.make_async_remote_copy(
            src_ref=send.at[c, d],
            dst_ref=recv.at[c, pl.ds(s * own, own)],
            send_sem=send_sem.at[c, d],
            recv_sem=recv_sem.at[c, s],
            device_id={"member": d},
            device_id_type=pl.DeviceIdType.MESH,
        )

    def back_piece(c, d, s):
        return pltpu.make_async_remote_copy(
            src_ref=back_send.at[c, d],
            dst_ref=back_recv.at[s, c],
            send_sem=back_send_sem.at[c, d],
            recv_sem=back_recv_sem.at[s, c],
            device_id={"member": d},
            device_id_type=pl.DeviceIdType.MESH,
        )

    token = lax.broadcasted_iota(jnp.int32, (tokens, tokens), 1)
    picked = jnp.where(arr_col_ref[...] == token, 1.0, 0.0).astype(BF16)
    order[...] = picked.reshape(n, chunks, ROWS, tokens)
    row_of = lax.broadcasted_iota(jnp.int32, table_ref.shape, 0)
    latent = lat_ref[...].astype(F32)
    for m in range(own):
        noise = jnp.sum(jnp.where(row_of == seed_ref[m], table_ref[...], 0.0), axis=0, keepdims=True)
        noisy[m] = (latent + pert_ref[m].astype(F32) * noise).astype(BF16)

    pl.semaphore_wait(barrier, n - 1)

    @pl.loop(0, chunks)
    def _(c):
        rows = order[:, c].reshape(n * ROWS, tokens)
        for m in range(own):
            send[c, :, m] = dot(rows, noisy[m]).astype(BF16).reshape(n, ROWS, width)
        for k in far_first:
            piece(c, lax.rem(me + k, n), me).start()
        recv[c, pl.ds(me * own, own)] = send[c, me]

    token = lax.broadcasted_iota(jnp.int32, (tokens, tokens), 0)
    order_t[...] = jnp.where(arr_row_ref[...] == token, 1.0, 0.0).astype(BF16)
    loads[0].wait()
    target[...] = dot(order[me].reshape(chunks * ROWS, tokens), tgt_ref[...]).reshape(
        chunks, ROWS, result
    )
    for load in loads[1:]:
        load.wait()

    def score(c):
        cells = members * PIECE_ITEMS
        left = lax.broadcasted_iota(jnp.int32, (cells, cells), 0)
        right = lax.broadcasted_iota(jnp.int32, (cells, cells), 1)
        same_item = left % PIECE_ITEMS == right % PIECE_ITEMS
        ones = jnp.where(left // PIECE_ITEMS == right // PIECE_ITEMS, 1.0, 0.0).astype(BF16)
        member_l = lax.broadcasted_iota(jnp.int32, (members, cells), 0)
        member_r = lax.broadcasted_iota(jnp.int32, (members, cells), 1)
        same_member = member_l == member_r // PIECE_ITEMS
        first_item = member_r % PIECE_ITEMS == 0
        for p in range(ROWS // PIECE_ITEMS):
            at = slice(p * PIECE_ITEMS, (p + 1) * PIECE_ITEMS)
            u3 = forecast[:, at, :]
            u = u3.reshape(cells, result)
            u16 = u.astype(BF16)
            products = jnp.where(same_item, dot(u16, u16, last=True), 0.0)
            by_item = jnp.sum(products.reshape(members, PIECE_ITEMS, cells), axis=1)
            gram = sum(dot(part, ones) for part in three_way(by_item))
            own_norm = jnp.sum(jnp.where(same_member & first_item, gram, 0.0), axis=1, keepdims=True)
            other_norm = jnp.sum(jnp.where(same_member, gram, 0.0), axis=0, keepdims=True)
            gap = jnp.where(same_member, 0.0, own_norm + other_norm - 2.0 * gram)
            weight = (1.0 / jnp.sqrt(gap + 1.0)).astype(BF16).astype(F32)
            total = jnp.sum(jnp.where(first_item, weight, 0.0), axis=1, keepdims=True)
            spread_out = jnp.broadcast_to(weight[:, None, :], (members, PIECE_ITEMS, cells))
            mixing = jnp.where(same_item, spread_out.reshape(cells, cells), 0.0).astype(BF16)
            weighted = dot(mixing, u16).reshape(members, PIECE_ITEMS, result)
            spread = (scale / members * (total[:, :, None] * u3 - weighted)).astype(BF16)
            miss = u3 - target[c, at, :][None]
            square = jnp.sum(miss * miss, axis=2, keepdims=True)
            norm = jnp.sqrt(jnp.sum(square, axis=1, keepdims=True) + 1.0)
            skill = miss / norm
            cotangent[:, at, :] = scale * skill - spread.astype(F32)

    @pl.loop(0, chunks)
    def _(c):
        for k in far_first:
            piece(c, me, lax.rem(me + k, n)).wait_recv()
        x = recv[c].reshape(members * ROWS, width)
        for h in range(0, hid, hid_tile):
            at = slice(h, h + hid_tile)
            gate = dot(x, wg_ref[:, at])
            up = dot(x, wu_ref[:, at])
            s = jax.nn.sigmoid(gate)
            gated = gate * s
            hidden[:, at] = (gated * up).astype(BF16)
            up_factor[:, at] = gated
            gate_factor[:, at] = up * (s + gated * (1.0 - s))
        value = dot(hidden[...], low_ref[...]).astype(BF16).astype(F32)
        forecast[...] = value.reshape(members, ROWS, result)
        score(c)
        ct = cotangent[...].reshape(members * ROWS, result).astype(BF16)
        for h in range(0, hid, hid_tile):
            at = slice(h, h + hid_tile)
            hidden_grad = dot(ct, low_ref[at, :], last=True)
            for i, factor in enumerate((gate_factor, up_factor)):
                grad = (hidden_grad * factor[:, at]).astype(BF16).astype(F32)
                total = jnp.sum(grad.reshape(members, ROWS, hid_tile), axis=0)
                high = total.astype(BF16)
                grads[i, :ROWS, at] = high
                grads[i, ROWS:, at] = (total - high.astype(F32)).astype(BF16)
        y = dot(grads[0], wg_ref[...], last=True) + dot(grads[1], wu_ref[...], last=True)
        y = y[:ROWS] + y[ROWS:]
        half = ROWS // 2
        for d in range(n):
            cols = slice(d * block, (d + 1) * block)
            parts = [y[:half, cols], y[half:, cols]]
            if 2 * block < LANES:
                parts.append(jnp.zeros((half, LANES - 2 * block), F32))
            back_send[c, d] = jnp.concatenate(parts, axis=1)
        for k in far_first:
            back_piece(c, lax.rem(me + k, n), me).start()
        back_recv[me, c] = back_send[c, me]

    @pl.loop(0, chunks)
    def _(c):
        for k in far_first:
            back_piece(c, me, lax.rem(me + k, n)).wait_recv()

    low_half = back_recv[...].reshape(n * chunks, 1, ROWS // 2, LANES)
    high_half = pltpu.roll(
        low_half.reshape(n * chunks * ROWS // 2, LANES), LANES - block, 1
    ).reshape(low_half.shape)
    patches = jnp.concatenate([low_half, high_half], axis=1).reshape(tokens, LANES)
    placed = sum(dot(order_t[...], part) for part in three_way(patches))
    out_ref[...] = placed[:, :block]

    @pl.loop(0, chunks)
    def _(c):
        for k in far_first:
            d = lax.rem(me + k, n)
            piece(c, d, me).wait_send()
            back_piece(c, d, me).wait_send()


def body(
    latents, sample_perturbation, noise_table, member_seed, piece_arrangement, targets,
    w_gate, w_up, lowering_matrix,
):
    n = lax.axis_size("member")
    own = sample_perturbation.shape[0]
    tokens, width = latents.shape
    hid, result = lowering_matrix.shape
    members = n * own
    chunks = tokens // (n * ROWS)
    block = width // n
    assert 2 * block <= LANES and chunks * n * ROWS == tokens == piece_arrangement.shape[0]
    vmem = pl.BlockSpec(memory_space=pltpu.VMEM)
    smem = pl.BlockSpec(memory_space=pltpu.SMEM)
    hbm = pl.BlockSpec(memory_space=pl.ANY)
    half = ROWS // 2
    rows = members * ROWS
    return pl.pallas_call(
        functools.partial(kernel, n, own, chunks, block, 256),
        out_shape=jax.ShapeDtypeStruct((tokens, block), F32),
        in_specs=[smem, vmem, vmem, vmem, vmem, vmem, hbm, hbm, hbm, hbm],
        out_specs=vmem,
        scratch_shapes=[
            pltpu.VMEM(targets.shape, BF16),
            pltpu.VMEM(w_gate.shape, BF16),
            pltpu.VMEM(w_up.shape, BF16),
            pltpu.VMEM(lowering_matrix.shape, BF16),
            pltpu.VMEM((n, chunks, ROWS, tokens), BF16),
            pltpu.VMEM((tokens, tokens), BF16),
            pltpu.VMEM((own, tokens, width), BF16),
            pltpu.VMEM((chunks, ROWS, result), F32),
            pltpu.VMEM((chunks, n, own, ROWS, width), BF16),
            pltpu.VMEM((chunks, members, ROWS, width), BF16),
            pltpu.VMEM((rows, hid), BF16),
            pltpu.VMEM((rows, hid), F32),
            pltpu.VMEM((rows, hid), F32),
            pltpu.VMEM((members, ROWS, result), F32),
            pltpu.VMEM((members, ROWS, result), F32),
            pltpu.VMEM((2, 2 * ROWS, hid), BF16),
            pltpu.VMEM((chunks, n, half, LANES), F32),
            pltpu.VMEM((n, chunks, half, LANES), F32),
            pltpu.SemaphoreType.DMA((4,)),
            pltpu.SemaphoreType.DMA((chunks, n)),
            pltpu.SemaphoreType.DMA((chunks, n)),
            pltpu.SemaphoreType.DMA((chunks, n)),
            pltpu.SemaphoreType.DMA((n, chunks)),
        ],
        compiler_params=pltpu.CompilerParams(
            collective_id=0, has_side_effects=True, vmem_limit_bytes=48 * 1024 * 1024
        ),
        name="energy_score_gradient",
    )(
        member_seed, latents, sample_perturbation, noise_table,
        piece_arrangement.reshape(1, tokens), piece_arrangement.reshape(tokens, 1),
        targets, w_gate, w_up, lowering_matrix,
    )


def solution(mesh):
    in_specs = (
        P("space", None),
        P("member", "space", None),
        P(),
        P("member"),
        P(),
        P("space", None),
        P(),
        P(),
        P(),
    )
    out_specs = P("space", "member")
    return jax.shard_map(body, mesh=mesh, in_specs=in_specs, out_specs=out_specs, check_vma=False)
```

```python
import functools

import jax
import jax.numpy as jnp
from jax import lax
from jax.experimental import pallas as pl
from jax.experimental.pallas import tpu as pltpu
from jax.sharding import PartitionSpec as P

PIECE_ITEMS = 8
ROWS = 16
LANES = 128
F32 = jnp.float32
BF16 = jnp.bfloat16


def dot(a, b, last=False):
    dims = (((1,), (1,)), ((), ())) if last else (((1,), (0,)), ((), ()))
    return lax.dot_general(a, b, dims, preferred_element_type=F32)


def three_way(x):
    high = x.astype(BF16)
    rest = x - high.astype(F32)
    mid = rest.astype(BF16)
    return high, mid, (rest - mid.astype(F32)).astype(BF16)


def kernel(
    n, own, chunks, block, hid_tile,
    seed_ref, arr_hbm, lat_hbm, table_hbm, pert_hbm, tgt_hbm, wg_hbm, wu_hbm, low_hbm,
    out_ref,
    arr_ref, lat_ref, table_ref, pert_ref, tgt_ref, wg_ref, wu_ref, low_ref,
    wg_t, wu_t, low_t,
    order, noisy, target, send, recv, hidden, gate_factor, up_factor, forecast, cotangent,
    grads, back_send, back_recv,
    load_sem, send_sem, recv_sem, back_send_sem, back_recv_sem,
):
    me = lax.axis_index("member")
    tokens, width = lat_ref.shape
    members = n * own
    hid = wg_ref.shape[1]
    result = low_ref.shape[1]
    scale = float(PIECE_ITEMS * result) ** 0.5
    far_first = sorted(range(1, n), key=lambda k: abs(k - n // 2))

    barrier = pltpu.get_barrier_semaphore()
    for k in range(1, n):
        pl.semaphore_signal(
            barrier, inc=1, device_id={"member": lax.rem(me + k, n)},
            device_id_type=pl.DeviceIdType.MESH,
        )
    loads = [
        pltpu.make_async_copy(src, dst, load_sem.at[i])
        for i, (src, dst) in enumerate(
            [(arr_hbm, arr_ref), (lat_hbm, lat_ref), (table_hbm, table_ref)]
            + [(pert_hbm.at[m], pert_ref.at[m]) for m in range(own)]
            + [(tgt_hbm, tgt_ref), (wg_hbm, wg_ref), (wu_hbm, wu_ref), (low_hbm, low_ref)]
        )
    ]
    for load in loads:
        load.start()

    def piece(c, d, s):
        return pltpu.make_async_remote_copy(
            src_ref=send.at[c, d],
            dst_ref=recv.at[c, pl.ds(s * own, own)],
            send_sem=send_sem.at[c, d],
            recv_sem=recv_sem.at[c, s],
            device_id={"member": d},
            device_id_type=pl.DeviceIdType.MESH,
        )

    def back_piece(c, d, s):
        return pltpu.make_async_remote_copy(
            src_ref=back_send.at[c, d],
            dst_ref=back_recv.at[s, c],
            send_sem=back_send_sem.at[c, d],
            recv_sem=back_recv_sem.at[s, c],
            device_id={"member": d},
            device_id_type=pl.DeviceIdType.MESH,
        )

    loads[0].wait()
    arr_row = arr_ref[...].reshape(1, tokens)
    arr_col = jnp.transpose(jnp.broadcast_to(arr_row, (8, tokens)))[:, :1]
    token = lax.broadcasted_iota(jnp.int32, (tokens, tokens), 1)
    picked = jnp.where(arr_col == token, 1.0, 0.0).astype(BF16)
    order[...] = picked.reshape(n, chunks, ROWS, tokens)
    loads[1].wait()
    loads[2].wait()
    row_of = lax.broadcasted_iota(jnp.int32, table_ref.shape, 0)
    latent = lat_ref[...].astype(F32)
    for m in range(own):
        loads[3 + m].wait()
        noise = jnp.sum(jnp.where(row_of == seed_ref[m], table_ref[...], 0.0), axis=0, keepdims=True)
        noisy[m] = (latent + pert_ref[m].astype(F32) * noise).astype(BF16)

    pl.semaphore_wait(barrier, n - 1)

    @pl.loop(0, chunks)
    def _(c):
        rows = order[:, c].reshape(n * ROWS, tokens)
        for m in range(own):
            send[c, :, m] = dot(rows, noisy[m]).astype(BF16).reshape(n, ROWS, width)
        for k in far_first:
            piece(c, lax.rem(me + k, n), me).start()
        recv[c, pl.ds(me * own, own)] = send[c, me]

    loads[3 + own].wait()
    target[...] = dot(order[me].reshape(chunks * ROWS, tokens), tgt_ref[...]).reshape(
        chunks, ROWS, result
    )
    for load in loads[4 + own :]:
        load.wait()
    wg_t[...] = jnp.transpose(wg_ref[...])
    wu_t[...] = jnp.transpose(wu_ref[...])
    low_t[...] = jnp.transpose(low_ref[...])

    def score(c):
        cells = members * PIECE_ITEMS
        left = lax.broadcasted_iota(jnp.int32, (cells, cells), 0)
        right = lax.broadcasted_iota(jnp.int32, (cells, cells), 1)
        same_item = left % PIECE_ITEMS == right % PIECE_ITEMS
        ones = jnp.where(left // PIECE_ITEMS == right // PIECE_ITEMS, 1.0, 0.0).astype(BF16)
        member_l = lax.broadcasted_iota(jnp.int32, (members, cells), 0)
        member_r = lax.broadcasted_iota(jnp.int32, (members, cells), 1)
        same_member = member_l == member_r // PIECE_ITEMS
        first_item = member_r % PIECE_ITEMS == 0
        for p in range(ROWS // PIECE_ITEMS):
            at = slice(p * PIECE_ITEMS, (p + 1) * PIECE_ITEMS)
            u3 = forecast[:, at, :]
            u = u3.reshape(cells, result)
            u16 = u.astype(BF16)
            products = jnp.where(same_item, dot(u16, u16, last=True), 0.0)
            by_item = jnp.sum(products.reshape(members, PIECE_ITEMS, cells), axis=1)
            gram = sum(dot(part, ones) for part in three_way(by_item))
            own_norm = jnp.sum(jnp.where(same_member & first_item, gram, 0.0), axis=1, keepdims=True)
            other_norm = jnp.sum(jnp.where(same_member, gram, 0.0), axis=0, keepdims=True)
            gap = jnp.where(same_member, 0.0, own_norm + other_norm - 2.0 * gram)
            weight = (1.0 / jnp.sqrt(gap + 1.0)).astype(BF16).astype(F32)
            total = jnp.sum(jnp.where(first_item, weight, 0.0), axis=1, keepdims=True)
            spread_out = jnp.broadcast_to(weight[:, None, :], (members, PIECE_ITEMS, cells))
            mixing = jnp.where(same_item, spread_out.reshape(cells, cells), 0.0).astype(BF16)
            weighted = dot(mixing, u16).reshape(members, PIECE_ITEMS, result)
            spread = (scale / members * (total[:, :, None] * u3 - weighted)).astype(BF16)
            miss = u3 - target[c, at, :][None]
            square = jnp.sum(miss * miss, axis=2, keepdims=True)
            norm = jnp.sqrt(jnp.sum(square, axis=1, keepdims=True) + 1.0)
            skill = miss / norm
            cotangent[:, at, :] = scale * skill - spread.astype(F32)

    @pl.loop(0, chunks)
    def _(c):
        for k in far_first:
            piece(c, me, lax.rem(me + k, n)).wait_recv()
        x = recv[c].reshape(members * ROWS, width)
        for h in range(0, hid, hid_tile):
            at = slice(h, h + hid_tile)
            gate = dot(x, wg_ref[:, at])
            up = dot(x, wu_ref[:, at])
            s = jax.nn.sigmoid(gate)
            gated = gate * s
            hidden[:, at] = (gated * up).astype(BF16)
            up_factor[:, at] = gated
            gate_factor[:, at] = up * (s + gated * (1.0 - s))
        value = dot(hidden[...], low_ref[...]).astype(BF16).astype(F32)
        forecast[...] = value.reshape(members, ROWS, result)
        score(c)
        ct = cotangent[...].reshape(members * ROWS, result).astype(BF16)
        for h in range(0, hid, hid_tile):
            at = slice(h, h + hid_tile)
            hidden_grad = dot(ct, low_t[:, at])
            for i, factor in enumerate((gate_factor, up_factor)):
                grad = (hidden_grad * factor[:, at]).astype(BF16).astype(F32)
                total = jnp.sum(grad.reshape(members, ROWS, hid_tile), axis=0)
                high = total.astype(BF16)
                grads[i, :ROWS, at] = high
                grads[i, ROWS:, at] = (total - high.astype(F32)).astype(BF16)
        y = dot(grads[0], wg_t[...]) + dot(grads[1], wu_t[...])
        y = y[:ROWS] + y[ROWS:]
        half = ROWS // 2
        for d in range(n):
            cols = slice(d * block, (d + 1) * block)
            parts = [y[:half, cols], y[half:, cols]]
            if 2 * block < LANES:
                parts.append(jnp.zeros((half, LANES - 2 * block), F32))
            back_send[c, d] = jnp.concatenate(parts, axis=1)
        for k in far_first:
            back_piece(c, lax.rem(me + k, n), me).start()
        back_recv[me, c] = back_send[c, me]

    @pl.loop(0, chunks)
    def _(c):
        for k in far_first:
            back_piece(c, me, lax.rem(me + k, n)).wait_recv()

    low_half = back_recv[...].reshape(n * chunks, 1, ROWS // 2, LANES)
    high_half = pltpu.roll(
        low_half.reshape(n * chunks * ROWS // 2, LANES), LANES - block, 1
    ).reshape(low_half.shape)
    patches = jnp.concatenate([low_half, high_half], axis=1).reshape(tokens, LANES)
    by_channel = jnp.transpose(patches)[:block]
    picks = order[...].reshape(tokens, tokens)
    out_ref[...] = sum(dot(part, picks) for part in three_way(by_channel))

    @pl.loop(0, chunks)
    def _(c):
        for k in far_first:
            d = lax.rem(me + k, n)
            piece(c, d, me).wait_send()
            back_piece(c, d, me).wait_send()


def body(
    latents, sample_perturbation, noise_table, member_seed, piece_arrangement, targets,
    w_gate, w_up, lowering_matrix,
):
    n = lax.axis_size("member")
    own = sample_perturbation.shape[0]
    tokens, width = latents.shape
    hid, result = lowering_matrix.shape
    members = n * own
    chunks = tokens // (n * ROWS)
    block = width // n
    assert 2 * block <= LANES and chunks * n * ROWS == tokens == piece_arrangement.shape[0]
    vmem = pl.BlockSpec(memory_space=pltpu.VMEM)
    smem = pl.BlockSpec(memory_space=pltpu.SMEM)
    hbm = pl.BlockSpec(memory_space=pl.ANY)
    half = ROWS // 2
    rows = members * ROWS
    return pl.pallas_call(
        functools.partial(kernel, n, own, chunks, block, 256),
        out_shape=jax.ShapeDtypeStruct((block, tokens), F32),
        in_specs=[smem] + [hbm] * 8,
        out_specs=vmem,
        scratch_shapes=[
            pltpu.VMEM(piece_arrangement.shape, jnp.int32),
            pltpu.VMEM(latents.shape, BF16),
            pltpu.VMEM(noise_table.shape, F32),
            pltpu.VMEM(sample_perturbation.shape, BF16),
            pltpu.VMEM(targets.shape, BF16),
            pltpu.VMEM(w_gate.shape, BF16),
            pltpu.VMEM(w_up.shape, BF16),
            pltpu.VMEM(lowering_matrix.shape, BF16),
            pltpu.VMEM((hid, width), BF16),
            pltpu.VMEM((hid, width), BF16),
            pltpu.VMEM((result, hid), BF16),
            pltpu.VMEM((n, chunks, ROWS, tokens), BF16),
            pltpu.VMEM((own, tokens, width), BF16),
            pltpu.VMEM((chunks, ROWS, result), F32),
            pltpu.VMEM((chunks, n, own, ROWS, width), BF16),
            pltpu.VMEM((chunks, members, ROWS, width), BF16),
            pltpu.VMEM((rows, hid), BF16),
            pltpu.VMEM((rows, hid), F32),
            pltpu.VMEM((rows, hid), F32),
            pltpu.VMEM((members, ROWS, result), F32),
            pltpu.VMEM((members, ROWS, result), F32),
            pltpu.VMEM((2, 2 * ROWS, hid), BF16),
            pltpu.VMEM((chunks, n, half, LANES), F32),
            pltpu.VMEM((n, chunks, half, LANES), F32),
            pltpu.SemaphoreType.DMA((7 + own,)),
            pltpu.SemaphoreType.DMA((chunks, n)),
            pltpu.SemaphoreType.DMA((chunks, n)),
            pltpu.SemaphoreType.DMA((chunks, n)),
            pltpu.SemaphoreType.DMA((n, chunks)),
        ],
        compiler_params=pltpu.CompilerParams(
            collective_id=0, has_side_effects=True, vmem_limit_bytes=64 * 1024 * 1024
        ),
        name="energy_score_gradient",
    )(
        member_seed, piece_arrangement, latents, noise_table, sample_perturbation,
        targets, w_gate, w_up, lowering_matrix,
    ).T


def solution(mesh):
    in_specs = (
        P("space", None),
        P("member", "space", None),
        P(),
        P("member"),
        P(),
        P("space", None),
        P(),
        P(),
        P(),
    )
    out_specs = P("space", "member")
    return jax.shard_map(body, mesh=mesh, in_specs=in_specs, out_specs=out_specs, check_vma=False)
```

```python
import functools

import jax
import jax.numpy as jnp
from jax import lax
from jax.experimental import pallas as pl
from jax.experimental.pallas import tpu as pltpu
from jax.sharding import PartitionSpec as P

PIECE_ITEMS = 8
ROWS = 16
LANES = 128
AHEAD = 2
F32 = jnp.float32
BF16 = jnp.bfloat16


def dot(a, b, last=False):
    dims = (((1,), (1,)), ((), ())) if last else (((1,), (0,)), ((), ()))
    return lax.dot_general(a, b, dims, preferred_element_type=F32)


def three_way(x):
    high = x.astype(BF16)
    rest = x - high.astype(F32)
    mid = rest.astype(BF16)
    return high, mid, (rest - mid.astype(F32)).astype(BF16)


def kernel(
    n, own, chunks, block, hid_tile,
    seed_ref, arr_hbm, lat_hbm, table_hbm, pert_hbm, tgt_hbm, wg_hbm, wu_hbm, low_hbm,
    out_ref,
    arr_ref, lat_ref, table_ref, pert_ref, tgt_ref, wg_ref, wu_ref, low_ref,
    wg_t, wu_t, low_t,
    order, noisy, target, send, recv, hidden, gate_factor, up_factor, forecast, cotangent,
    grads, back_send, back_recv,
    load_sem, send_sem, recv_sem, back_send_sem, back_recv_sem,
):
    me = lax.axis_index("member")
    tokens, width = lat_ref.shape
    members = n * own
    hid = wg_ref.shape[1]
    result = low_ref.shape[1]
    scale = float(PIECE_ITEMS * result) ** 0.5
    far_first = sorted(range(1, n), key=lambda k: abs(k - n // 2))

    barrier = pltpu.get_barrier_semaphore()
    for k in range(1, n):
        pl.semaphore_signal(
            barrier, inc=1, device_id={"member": lax.rem(me + k, n)},
            device_id_type=pl.DeviceIdType.MESH,
        )
    loads = [
        pltpu.make_async_copy(src, dst, load_sem.at[i])
        for i, (src, dst) in enumerate(
            [(arr_hbm, arr_ref), (lat_hbm, lat_ref), (table_hbm, table_ref)]
            + [(pert_hbm.at[m], pert_ref.at[m]) for m in range(own)]
            + [(tgt_hbm, tgt_ref), (wg_hbm, wg_ref), (wu_hbm, wu_ref), (low_hbm, low_ref)]
        )
    ]
    for load in loads:
        load.start()

    def piece(c, d, s):
        return pltpu.make_async_remote_copy(
            src_ref=send.at[c, d],
            dst_ref=recv.at[c, pl.ds(s * own, own)],
            send_sem=send_sem.at[c, d],
            recv_sem=recv_sem.at[c, s],
            device_id={"member": d},
            device_id_type=pl.DeviceIdType.MESH,
        )

    def back_piece(c, d, s):
        return pltpu.make_async_remote_copy(
            src_ref=back_send.at[c, d],
            dst_ref=back_recv.at[s, c],
            send_sem=back_send_sem.at[c, d],
            recv_sem=back_recv_sem.at[s, c],
            device_id={"member": d},
            device_id_type=pl.DeviceIdType.MESH,
        )

    loads[0].wait()
    arr_row = arr_ref[...].reshape(1, tokens)
    arr_col = jnp.transpose(jnp.broadcast_to(arr_row, (8, tokens)))[:, :1]
    token = lax.broadcasted_iota(jnp.int32, (tokens, tokens), 1)
    picked = jnp.where(arr_col == token, 1.0, 0.0).astype(BF16)
    order[...] = picked.reshape(n, chunks, ROWS, tokens)
    loads[1].wait()
    loads[2].wait()
    row_of = lax.broadcasted_iota(jnp.int32, table_ref.shape, 0)
    latent = lat_ref[...].astype(F32)
    for m in range(own):
        loads[3 + m].wait()
        noise = jnp.sum(jnp.where(row_of == seed_ref[m], table_ref[...], 0.0), axis=0, keepdims=True)
        noisy[m] = (latent + pert_ref[m].astype(F32) * noise).astype(BF16)

    pl.semaphore_wait(barrier, n - 1)

    def dispatch(c):
        rows = order[:, c].reshape(n * ROWS, tokens)
        for m in range(own):
            send[c, :, m] = dot(rows, noisy[m]).astype(BF16).reshape(n, ROWS, width)
        for k in far_first:
            piece(c, lax.rem(me + k, n), me).start()
        recv[c, pl.ds(me * own, own)] = send[c, me]

    ahead = min(AHEAD, chunks)
    pl.loop(0, ahead)(dispatch)

    loads[3 + own].wait()
    target[...] = dot(order[me].reshape(chunks * ROWS, tokens), tgt_ref[...]).reshape(
        chunks, ROWS, result
    )
    for load in loads[4 + own :]:
        load.wait()
    wg_t[...] = jnp.transpose(wg_ref[...])
    wu_t[...] = jnp.transpose(wu_ref[...])
    low_t[...] = jnp.transpose(low_ref[...])

    def score(c):
        cells = members * PIECE_ITEMS
        left = lax.broadcasted_iota(jnp.int32, (cells, cells), 0)
        right = lax.broadcasted_iota(jnp.int32, (cells, cells), 1)
        same_item = left % PIECE_ITEMS == right % PIECE_ITEMS
        ones = jnp.where(left // PIECE_ITEMS == right // PIECE_ITEMS, 1.0, 0.0).astype(BF16)
        member_l = lax.broadcasted_iota(jnp.int32, (members, cells), 0)
        member_r = lax.broadcasted_iota(jnp.int32, (members, cells), 1)
        same_member = member_l == member_r // PIECE_ITEMS
        first_item = member_r % PIECE_ITEMS == 0
        for p in range(ROWS // PIECE_ITEMS):
            at = slice(p * PIECE_ITEMS, (p + 1) * PIECE_ITEMS)
            u3 = forecast[:, at, :]
            u = u3.reshape(cells, result)
            u16 = u.astype(BF16)
            products = jnp.where(same_item, dot(u16, u16, last=True), 0.0)
            by_item = jnp.sum(products.reshape(members, PIECE_ITEMS, cells), axis=1)
            gram = sum(dot(part, ones) for part in three_way(by_item))
            own_norm = jnp.sum(jnp.where(same_member & first_item, gram, 0.0), axis=1, keepdims=True)
            other_norm = jnp.sum(jnp.where(same_member, gram, 0.0), axis=0, keepdims=True)
            gap = jnp.where(same_member, 0.0, own_norm + other_norm - 2.0 * gram)
            weight = (1.0 / jnp.sqrt(gap + 1.0)).astype(BF16).astype(F32)
            total = jnp.sum(jnp.where(first_item, weight, 0.0), axis=1, keepdims=True)
            spread_out = jnp.broadcast_to(weight[:, None, :], (members, PIECE_ITEMS, cells))
            mixing = jnp.where(same_item, spread_out.reshape(cells, cells), 0.0).astype(BF16)
            weighted = dot(mixing, u16).reshape(members, PIECE_ITEMS, result)
            spread = (scale / members * (total[:, :, None] * u3 - weighted)).astype(BF16)
            miss = u3 - target[c, at, :][None]
            square = jnp.sum(miss * miss, axis=2, keepdims=True)
            norm = jnp.sqrt(jnp.sum(square, axis=1, keepdims=True) + 1.0)
            skill = miss / norm
            cotangent[:, at, :] = scale * skill - spread.astype(F32)

    @pl.loop(0, chunks)
    def _(c):
        for k in far_first:
            piece(c, me, lax.rem(me + k, n)).wait_recv()

        @pl.when(c + ahead < chunks)
        def _():
            dispatch(c + ahead)

        x = recv[c].reshape(members * ROWS, width)
        for h in range(0, hid, hid_tile):
            at = slice(h, h + hid_tile)
            gate = dot(x, wg_ref[:, at])
            up = dot(x, wu_ref[:, at])
            s = jax.nn.sigmoid(gate)
            gated = gate * s
            hidden[:, at] = (gated * up).astype(BF16)
            up_factor[:, at] = gated
            gate_factor[:, at] = up * (s + gated * (1.0 - s))
        value = dot(hidden[...], low_ref[...]).astype(BF16).astype(F32)
        forecast[...] = value.reshape(members, ROWS, result)
        score(c)
        ct = cotangent[...].reshape(members * ROWS, result).astype(BF16)
        for h in range(0, hid, hid_tile):
            at = slice(h, h + hid_tile)
            hidden_grad = dot(ct, low_t[:, at])
            for i, factor in enumerate((gate_factor, up_factor)):
                grad = (hidden_grad * factor[:, at]).astype(BF16).astype(F32)
                total = jnp.sum(grad.reshape(members, ROWS, hid_tile), axis=0)
                high = total.astype(BF16)
                grads[i, :ROWS, at] = high
                grads[i, ROWS:, at] = (total - high.astype(F32)).astype(BF16)
        y = dot(grads[0], wg_t[...]) + dot(grads[1], wu_t[...])
        y = y[:ROWS] + y[ROWS:]
        half = ROWS // 2
        for d in range(n):
            cols = slice(d * block, (d + 1) * block)
            parts = [y[:half, cols], y[half:, cols]]
            if 2 * block < LANES:
                parts.append(jnp.zeros((half, LANES - 2 * block), F32))
            back_send[c, d] = jnp.concatenate(parts, axis=1)
        for k in far_first:
            back_piece(c, lax.rem(me + k, n), me).start()
        back_recv[me, c] = back_send[c, me]

    @pl.loop(0, chunks)
    def _(c):
        for k in far_first:
            back_piece(c, me, lax.rem(me + k, n)).wait_recv()

    low_half = back_recv[...].reshape(n * chunks, 1, ROWS // 2, LANES)
    high_half = pltpu.roll(
        low_half.reshape(n * chunks * ROWS // 2, LANES), LANES - block, 1
    ).reshape(low_half.shape)
    patches = jnp.concatenate([low_half, high_half], axis=1).reshape(tokens, LANES)
    by_channel = jnp.transpose(patches)[:block]
    picks = order[...].reshape(tokens, tokens)
    out_ref[...] = jnp.transpose(sum(dot(part, picks) for part in three_way(by_channel)))

    @pl.loop(0, chunks)
    def _(c):
        for k in far_first:
            d = lax.rem(me + k, n)
            piece(c, d, me).wait_send()
            back_piece(c, d, me).wait_send()


def body(
    latents, sample_perturbation, noise_table, member_seed, piece_arrangement, targets,
    w_gate, w_up, lowering_matrix,
):
    n = lax.axis_size("member")
    own = sample_perturbation.shape[0]
    tokens, width = latents.shape
    hid, result = lowering_matrix.shape
    members = n * own
    chunks = tokens // (n * ROWS)
    block = width // n
    assert 2 * block <= LANES and chunks * n * ROWS == tokens == piece_arrangement.shape[0]
    vmem = pl.BlockSpec(memory_space=pltpu.VMEM)
    smem = pl.BlockSpec(memory_space=pltpu.SMEM)
    hbm = pl.BlockSpec(memory_space=pl.ANY)
    half = ROWS // 2
    rows = members * ROWS
    return pl.pallas_call(
        functools.partial(kernel, n, own, chunks, block, 256),
        out_shape=jax.ShapeDtypeStruct((tokens, block), F32),
        in_specs=[smem] + [hbm] * 8,
        out_specs=vmem,
        scratch_shapes=[
            pltpu.VMEM(piece_arrangement.shape, jnp.int32),
            pltpu.VMEM(latents.shape, BF16),
            pltpu.VMEM(noise_table.shape, F32),
            pltpu.VMEM(sample_perturbation.shape, BF16),
            pltpu.VMEM(targets.shape, BF16),
            pltpu.VMEM(w_gate.shape, BF16),
            pltpu.VMEM(w_up.shape, BF16),
            pltpu.VMEM(lowering_matrix.shape, BF16),
            pltpu.VMEM((hid, width), BF16),
            pltpu.VMEM((hid, width), BF16),
            pltpu.VMEM((result, hid), BF16),
            pltpu.VMEM((n, chunks, ROWS, tokens), BF16),
            pltpu.VMEM((own, tokens, width), BF16),
            pltpu.VMEM((chunks, ROWS, result), F32),
            pltpu.VMEM((chunks, n, own, ROWS, width), BF16),
            pltpu.VMEM((chunks, members, ROWS, width), BF16),
            pltpu.VMEM((rows, hid), BF16),
            pltpu.VMEM((rows, hid), F32),
            pltpu.VMEM((rows, hid), F32),
            pltpu.VMEM((members, ROWS, result), F32),
            pltpu.VMEM((members, ROWS, result), F32),
            pltpu.VMEM((2, 2 * ROWS, hid), BF16),
            pltpu.VMEM((chunks, n, half, LANES), F32),
            pltpu.VMEM((n, chunks, half, LANES), F32),
            pltpu.SemaphoreType.DMA((7 + own,)),
            pltpu.SemaphoreType.DMA((chunks, n)),
            pltpu.SemaphoreType.DMA((chunks, n)),
            pltpu.SemaphoreType.DMA((chunks, n)),
            pltpu.SemaphoreType.DMA((n, chunks)),
        ],
        compiler_params=pltpu.CompilerParams(
            collective_id=0, has_side_effects=True, vmem_limit_bytes=64 * 1024 * 1024
        ),
        name="energy_score_gradient",
    )(
        member_seed, piece_arrangement, latents, noise_table, sample_perturbation,
        targets, w_gate, w_up, lowering_matrix,
    )


def solution(mesh):
    in_specs = (
        P("space", None),
        P("member", "space", None),
        P(),
        P("member"),
        P(),
        P("space", None),
        P(),
        P(),
        P(),
    )
    out_specs = P("space", "member")
    return jax.shard_map(body, mesh=mesh, in_specs=in_specs, out_specs=out_specs, check_vma=False)
```

```python
import functools

import jax
import jax.numpy as jnp
from jax import lax
from jax.experimental import pallas as pl
from jax.experimental.pallas import tpu as pltpu
from jax.sharding import PartitionSpec as P

PIECE_ITEMS = 8
ROWS = 16
LANES = 128
F32 = jnp.float32
BF16 = jnp.bfloat16


def dot(a, b, last=False):
    dims = (((1,), (1,)), ((), ())) if last else (((1,), (0,)), ((), ()))
    return lax.dot_general(a, b, dims, preferred_element_type=F32)


def three_way(x):
    high = x.astype(BF16)
    rest = x - high.astype(F32)
    mid = rest.astype(BF16)
    return high, mid, (rest - mid.astype(F32)).astype(BF16)


def kernel(
    n, own, chunks, block, hid_tile,
    seed_ref, arr_hbm, lat_hbm, table_hbm, pert_hbm, tgt_hbm, wg_hbm, wu_hbm, low_hbm,
    out_ref,
    arr_ref, lat_ref, table_ref, pert_ref, tgt_ref, wg_ref, wu_ref, low_ref,
    wg_t, wu_t, low_t,
    order, noisy, target, send, recv, hidden, gate_factor, up_factor, forecast, cotangent,
    grads, same_item, ones, same_member, back_send, back_recv,
    load_sem, send_sem, recv_sem, back_send_sem, back_recv_sem,
):
    me = lax.axis_index("member")
    tokens, width = lat_ref.shape
    members = n * own
    hid = wg_ref.shape[1]
    result = low_ref.shape[1]
    scale = float(PIECE_ITEMS * result) ** 0.5
    far_first = sorted(range(1, n), key=lambda k: abs(k - n // 2))

    barrier = pltpu.get_barrier_semaphore()
    for k in range(1, n):
        pl.semaphore_signal(
            barrier, inc=1, device_id={"member": lax.rem(me + k, n)},
            device_id_type=pl.DeviceIdType.MESH,
        )
    loads = [
        pltpu.make_async_copy(src, dst, load_sem.at[i])
        for i, (src, dst) in enumerate(
            [(arr_hbm, arr_ref), (lat_hbm, lat_ref), (table_hbm, table_ref)]
            + [(pert_hbm.at[m], pert_ref.at[m]) for m in range(own)]
            + [(tgt_hbm, tgt_ref), (wg_hbm, wg_ref), (wu_hbm, wu_ref), (low_hbm, low_ref)]
        )
    ]
    for load in loads:
        load.start()

    def piece(c, d, s):
        return pltpu.make_async_remote_copy(
            src_ref=send.at[c, d],
            dst_ref=recv.at[c, pl.ds(s * own, own)],
            send_sem=send_sem.at[c, d],
            recv_sem=recv_sem.at[c, s],
            device_id={"member": d},
            device_id_type=pl.DeviceIdType.MESH,
        )

    def back_piece(c, d, s):
        return pltpu.make_async_remote_copy(
            src_ref=back_send.at[c, d],
            dst_ref=back_recv.at[s, c],
            send_sem=back_send_sem.at[c, d],
            recv_sem=back_recv_sem.at[s, c],
            device_id={"member": d},
            device_id_type=pl.DeviceIdType.MESH,
        )

    loads[0].wait()
    arr_row = arr_ref[...].reshape(1, tokens)
    arr_col = jnp.transpose(jnp.broadcast_to(arr_row, (8, tokens)))[:, :1]
    token = lax.broadcasted_iota(jnp.int32, (tokens, tokens), 1)
    picked = jnp.where(arr_col == token, 1.0, 0.0).astype(BF16)
    order[...] = picked.reshape(n, chunks, ROWS, tokens)
    loads[1].wait()
    loads[2].wait()
    row_of = lax.broadcasted_iota(jnp.int32, table_ref.shape, 0)
    latent = lat_ref[...].astype(F32)
    for m in range(own):
        loads[3 + m].wait()
        noise = jnp.sum(jnp.where(row_of == seed_ref[m], table_ref[...], 0.0), axis=0, keepdims=True)
        noisy[m] = (latent + pert_ref[m].astype(F32) * noise).astype(BF16)

    pl.semaphore_wait(barrier, n - 1)

    def dispatch(c):
        rows = order[:, c].reshape(n * ROWS, tokens)
        for m in range(own):
            send[c, :, m] = dot(rows, noisy[m]).astype(BF16).reshape(n, ROWS, width)
        for k in far_first:
            piece(c, lax.rem(me + k, n), me).start()
        recv[c, pl.ds(me * own, own)] = send[c, me]

    pl.loop(0, chunks)(dispatch)

    loads[3 + own].wait()
    target[...] = dot(order[me].reshape(chunks * ROWS, tokens), tgt_ref[...]).reshape(
        chunks, ROWS, result
    )
    for load in loads[4 + own :]:
        load.wait()
    wg_t[...] = jnp.transpose(wg_ref[...])
    wu_t[...] = jnp.transpose(wu_ref[...])
    low_t[...] = jnp.transpose(low_ref[...])

    cells = members * PIECE_ITEMS
    left = lax.broadcasted_iota(jnp.int32, (cells, cells), 0)
    right = lax.broadcasted_iota(jnp.int32, (cells, cells), 1)
    same_item[...] = jnp.where((left & (PIECE_ITEMS - 1)) == (right & (PIECE_ITEMS - 1)), 1.0, 0.0)
    ones[...] = jnp.where(left // PIECE_ITEMS == right // PIECE_ITEMS, 1.0, 0.0).astype(BF16)
    member_l = lax.broadcasted_iota(jnp.int32, (members, cells), 0)
    member_r = lax.broadcasted_iota(jnp.int32, (members, cells), 1)
    same_member[...] = jnp.where(member_l == member_r // PIECE_ITEMS, 1.0, 0.0)

    def score(c):
        patches = [slice(p, p + PIECE_ITEMS) for p in range(0, ROWS, PIECE_ITEMS)]
        us = [forecast[:, at, :].reshape(cells, result) for at in patches]
        narrow = [u.astype(BF16) for u in us]
        by_item = jnp.concatenate(
            [
                jnp.sum((dot(u, u, last=True) * same_item[...]).reshape(members, PIECE_ITEMS, cells), axis=1)
                for u in narrow
            ],
            axis=0,
        )
        count = by_item.shape[0]
        grams = dot(jnp.concatenate(three_way(by_item), axis=0), ones[...])
        gram = (grams[:count] + grams[count : 2 * count] + grams[2 * count :]).reshape(
            len(patches), members, cells
        )
        mine = same_member[...][None]
        diagonal = gram * mine
        own_norm = jnp.sum(diagonal, axis=2, keepdims=True) * (1.0 / PIECE_ITEMS)
        other_norm = jnp.sum(diagonal, axis=1, keepdims=True)
        gap = (own_norm + other_norm - 2.0 * gram) * (1.0 - mine)
        weight = lax.rsqrt(gap + 1.0).astype(BF16).astype(F32)
        for p, at in enumerate(patches):
            u = us[p]
            spread_out = jnp.broadcast_to(weight[p][:, None, :], (members, PIECE_ITEMS, cells))
            mixing = spread_out.reshape(cells, cells) * same_item[...]
            total = jnp.sum(mixing, axis=1, keepdims=True)
            weighted = dot(mixing.astype(BF16), narrow[p])
            spread = (scale / members * (total * u - weighted)).astype(BF16)
            miss = (u.reshape(members, PIECE_ITEMS, result) - target[c, at, :][None]).reshape(u.shape)
            square = jnp.sum(miss * miss, axis=1, keepdims=True).reshape(members, PIECE_ITEMS, 1)
            norm = jnp.sqrt(jnp.sum(square, axis=1, keepdims=True) + 1.0)
            per_norm = jnp.broadcast_to(scale / norm, square.shape).reshape(cells, 1)
            cotangent[:, at, :] = (miss * per_norm - spread.astype(F32)).reshape(
                members, PIECE_ITEMS, result
            )

    @pl.loop(0, chunks)
    def _(c):
        for k in far_first:
            piece(c, me, lax.rem(me + k, n)).wait_recv()
        x = recv[c].reshape(members * ROWS, width)
        for h in range(0, hid, hid_tile):
            at = slice(h, h + hid_tile)
            gate = dot(x, wg_ref[:, at])
            up = dot(x, wu_ref[:, at])
            s = 0.5 * jnp.tanh(0.5 * gate) + 0.5
            gated = gate * s
            hidden[:, at] = (gated * up).astype(BF16)
            up_factor[:, at] = gated
            gate_factor[:, at] = up * (s + gated * (1.0 - s))
        value = dot(hidden[...], low_ref[...]).astype(BF16).astype(F32)
        forecast[...] = value.reshape(members, ROWS, result)
        score(c)
        ct = cotangent[...].reshape(members * ROWS, result).astype(BF16)
        for h in range(0, hid, hid_tile):
            at = slice(h, h + hid_tile)
            hidden_grad = dot(ct, low_t[:, at])
            for i, factor in enumerate((gate_factor, up_factor)):
                grad = (hidden_grad * factor[:, at]).astype(BF16).astype(F32)
                total = jnp.sum(grad.reshape(members, ROWS, hid_tile), axis=0)
                high = total.astype(BF16)
                grads[i, :ROWS, at] = high
                grads[i, ROWS:, at] = (total - high.astype(F32)).astype(BF16)
        y = dot(grads[0], wg_t[...]) + dot(grads[1], wu_t[...])
        y = y[:ROWS] + y[ROWS:]
        half = ROWS // 2
        for d in range(n):
            cols = slice(d * block, (d + 1) * block)
            parts = [y[:half, cols], y[half:, cols]]
            if 2 * block < LANES:
                parts.append(jnp.zeros((half, LANES - 2 * block), F32))
            back_send[c, d] = jnp.concatenate(parts, axis=1)
        for k in far_first:
            back_piece(c, lax.rem(me + k, n), me).start()
        back_recv[me, c] = back_send[c, me]

    @pl.loop(0, chunks)
    def _(c):
        for k in far_first:
            back_piece(c, me, lax.rem(me + k, n)).wait_recv()

    low_half = back_recv[...].reshape(n * chunks, 1, ROWS // 2, LANES)
    high_half = pltpu.roll(
        low_half.reshape(n * chunks * ROWS // 2, LANES), LANES - block, 1
    ).reshape(low_half.shape)
    patches = jnp.concatenate([low_half, high_half], axis=1).reshape(tokens, LANES)
    by_channel = jnp.transpose(patches)[:block]
    picks = order[...].reshape(tokens, tokens)
    out_ref[...] = jnp.transpose(sum(dot(part, picks) for part in three_way(by_channel)))

    @pl.loop(0, chunks)
    def _(c):
        for k in far_first:
            d = lax.rem(me + k, n)
            piece(c, d, me).wait_send()
            back_piece(c, d, me).wait_send()


def body(
    latents, sample_perturbation, noise_table, member_seed, piece_arrangement, targets,
    w_gate, w_up, lowering_matrix,
):
    n = lax.axis_size("member")
    own = sample_perturbation.shape[0]
    tokens, width = latents.shape
    hid, result = lowering_matrix.shape
    members = n * own
    chunks = tokens // (n * ROWS)
    block = width // n
    assert 2 * block <= LANES and chunks * n * ROWS == tokens == piece_arrangement.shape[0]
    vmem = pl.BlockSpec(memory_space=pltpu.VMEM)
    smem = pl.BlockSpec(memory_space=pltpu.SMEM)
    hbm = pl.BlockSpec(memory_space=pl.ANY)
    half = ROWS // 2
    rows = members * ROWS
    return pl.pallas_call(
        functools.partial(kernel, n, own, chunks, block, 256),
        out_shape=jax.ShapeDtypeStruct((tokens, block), F32),
        in_specs=[smem] + [hbm] * 8,
        out_specs=vmem,
        scratch_shapes=[
            pltpu.VMEM(piece_arrangement.shape, jnp.int32),
            pltpu.VMEM(latents.shape, BF16),
            pltpu.VMEM(noise_table.shape, F32),
            pltpu.VMEM(sample_perturbation.shape, BF16),
            pltpu.VMEM(targets.shape, BF16),
            pltpu.VMEM(w_gate.shape, BF16),
            pltpu.VMEM(w_up.shape, BF16),
            pltpu.VMEM(lowering_matrix.shape, BF16),
            pltpu.VMEM((hid, width), BF16),
            pltpu.VMEM((hid, width), BF16),
            pltpu.VMEM((result, hid), BF16),
            pltpu.VMEM((n, chunks, ROWS, tokens), BF16),
            pltpu.VMEM((own, tokens, width), BF16),
            pltpu.VMEM((chunks, ROWS, result), F32),
            pltpu.VMEM((chunks, n, own, ROWS, width), BF16),
            pltpu.VMEM((chunks, members, ROWS, width), BF16),
            pltpu.VMEM((rows, hid), BF16),
            pltpu.VMEM((rows, hid), F32),
            pltpu.VMEM((rows, hid), F32),
            pltpu.VMEM((members, ROWS, result), F32),
            pltpu.VMEM((members, ROWS, result), F32),
            pltpu.VMEM((2, 2 * ROWS, hid), BF16),
            pltpu.VMEM((members * PIECE_ITEMS, members * PIECE_ITEMS), F32),
            pltpu.VMEM((members * PIECE_ITEMS, members * PIECE_ITEMS), BF16),
            pltpu.VMEM((members, members * PIECE_ITEMS), F32),
            pltpu.VMEM((chunks, n, half, LANES), F32),
            pltpu.VMEM((n, chunks, half, LANES), F32),
            pltpu.SemaphoreType.DMA((7 + own,)),
            pltpu.SemaphoreType.DMA((chunks, n)),
            pltpu.SemaphoreType.DMA((chunks, n)),
            pltpu.SemaphoreType.DMA((chunks, n)),
            pltpu.SemaphoreType.DMA((n, chunks)),
        ],
        compiler_params=pltpu.CompilerParams(
            collective_id=0, has_side_effects=True, vmem_limit_bytes=64 * 1024 * 1024
        ),
        name="energy_score_gradient",
    )(
        member_seed, piece_arrangement, latents, noise_table, sample_perturbation,
        targets, w_gate, w_up, lowering_matrix,
    )


def solution(mesh):
    in_specs = (
        P("space", None),
        P("member", "space", None),
        P(),
        P("member"),
        P(),
        P("space", None),
        P(),
        P(),
        P(),
    )
    out_specs = P("space", "member")
    return jax.shard_map(body, mesh=mesh, in_specs=in_specs, out_specs=out_specs, check_vma=False)
```

```python
import functools

import jax
import jax.numpy as jnp
from jax import lax
from jax.experimental import pallas as pl
from jax.experimental.pallas import tpu as pltpu
from jax.sharding import PartitionSpec as P

PIECE_ITEMS = 8
ROWS = 16
LANES = 128
F32 = jnp.float32
BF16 = jnp.bfloat16


def dot(a, b, last=False):
    dims = (((1,), (1,)), ((), ())) if last else (((1,), (0,)), ((), ()))
    return lax.dot_general(a, b, dims, preferred_element_type=F32)


def three_way(x):
    high = x.astype(BF16)
    rest = x - high.astype(F32)
    mid = rest.astype(BF16)
    return high, mid, (rest - mid.astype(F32)).astype(BF16)


def kernel(
    n, own, chunks, block, hid_tile,
    seed_ref, arr_hbm, lat_hbm, table_hbm, pert_hbm, tgt_hbm, wg_hbm, wu_hbm, low_hbm,
    out_ref,
    arr_ref, lat_ref, table_ref, pert_ref, tgt_ref, wg_ref, wu_ref, low_ref,
    wg_t, wu_t, low_t,
    order, order_t, noisy, target, send, recv, hidden, gate_factor, up_factor, forecast, cotangent,
    grads, same_item, ones, same_member, pair, back_send, back_recv,
    load_sem, send_sem, recv_sem, first_send_sem, first_recv_sem, back_send_sem, back_recv_sem,
):
    me = lax.axis_index("member")
    tokens, width = lat_ref.shape
    members = n * own
    hid = wg_ref.shape[1]
    result = low_ref.shape[1]
    scale = float(PIECE_ITEMS * result) ** 0.5
    far_first = sorted(range(1, n), key=lambda k: abs(k - n // 2))

    barrier = pltpu.get_barrier_semaphore()
    for k in range(1, n):
        pl.semaphore_signal(
            barrier, inc=1, device_id={"member": lax.rem(me + k, n)},
            device_id_type=pl.DeviceIdType.MESH,
        )
    loads = [
        pltpu.make_async_copy(src, dst, load_sem.at[i])
        for i, (src, dst) in enumerate(
            [(arr_hbm, arr_ref), (lat_hbm, lat_ref), (table_hbm, table_ref)]
            + [(pert_hbm.at[m], pert_ref.at[m]) for m in range(own)]
            + [(tgt_hbm, tgt_ref), (wg_hbm, wg_ref), (wu_hbm, wu_ref), (low_hbm, low_ref)]
        )
    ]
    for load in loads:
        load.start()

    def piece(c, d, s):
        return pltpu.make_async_remote_copy(
            src_ref=send.at[c, d],
            dst_ref=recv.at[c, pl.ds(s * own, own)],
            send_sem=send_sem.at[c, d],
            recv_sem=recv_sem.at[c, s],
            device_id={"member": d},
            device_id_type=pl.DeviceIdType.MESH,
        )

    def first_piece(m, d, s):
        return pltpu.make_async_remote_copy(
            src_ref=send.at[0, d, m],
            dst_ref=recv.at[0, s * own + m],
            send_sem=first_send_sem.at[m, d],
            recv_sem=first_recv_sem.at[m, s],
            device_id={"member": d},
            device_id_type=pl.DeviceIdType.MESH,
        )

    def back_piece(g, d, s):
        return pltpu.make_async_remote_copy(
            src_ref=back_send.at[g, d],
            dst_ref=back_recv.at[s, g],
            send_sem=back_send_sem.at[g, d],
            recv_sem=back_recv_sem.at[s, g],
            device_id={"member": d},
            device_id_type=pl.DeviceIdType.MESH,
        )

    loads[0].wait()
    arr_row = arr_ref[...].reshape(1, tokens)
    arr_col = jnp.transpose(jnp.broadcast_to(arr_row, (8, tokens)))[:, :1]
    def pick(c):
        token = lax.broadcasted_iota(jnp.int32, (n, ROWS, tokens), 2)
        place = arr_col.reshape(n, chunks, ROWS, 1)[:, c]
        order[:, c] = jnp.where(place == token, 1.0, 0.0).astype(BF16)

    pick(0)
    loads[1].wait()
    loads[2].wait()
    row_of = lax.broadcasted_iota(jnp.int32, table_ref.shape, 0)
    rows = order[:, 0].reshape(n * ROWS, tokens)
    for m in range(own):
        noise = jnp.sum(jnp.where(row_of == seed_ref[m], table_ref[...], 0.0), axis=0, keepdims=True)
        loads[3 + m].wait()
        noisy[m] = (lat_ref[...].astype(F32) + pert_ref[m].astype(F32) * noise).astype(BF16)
        send[0, :, m] = dot(rows, noisy[m]).astype(BF16).reshape(n, ROWS, width)
        if m == 0:
            pl.semaphore_wait(barrier, n - 1)
        for k in far_first:
            first_piece(m, lax.rem(me + k, n), me).start()
    recv[0, pl.ds(me * own, own)] = send[0, me]

    for c in range(1, chunks):
        pick(c)

    @pl.loop(1, chunks)
    def _(c):
        rows = order[:, c].reshape(n * ROWS, tokens)
        for m in range(own):
            send[c, :, m] = dot(rows, noisy[m]).astype(BF16).reshape(n, ROWS, width)
        for k in far_first:
            piece(c, lax.rem(me + k, n), me).start()
        recv[c, pl.ds(me * own, own)] = send[c, me]

    token = lax.broadcasted_iota(jnp.int32, (tokens, tokens), 0)
    order_t[...] = jnp.where(arr_row == token, 1.0, 0.0).astype(BF16)
    loads[3 + own].wait()
    target[...] = dot(order[me].reshape(chunks * ROWS, tokens), tgt_ref[...]).reshape(
        chunks, ROWS, result
    )
    for load in loads[4 + own :]:
        load.wait()
    wg_t[...] = jnp.transpose(wg_ref[...])
    wu_t[...] = jnp.transpose(wu_ref[...])
    low_t[...] = jnp.transpose(low_ref[...])

    cells = members * PIECE_ITEMS
    left = lax.broadcasted_iota(jnp.int32, (cells, cells), 0)
    right = lax.broadcasted_iota(jnp.int32, (cells, cells), 1)
    same_item[...] = jnp.where((left & (PIECE_ITEMS - 1)) == (right & (PIECE_ITEMS - 1)), 1.0, 0.0)
    ones[...] = jnp.where(left // PIECE_ITEMS == right // PIECE_ITEMS, 1.0, 0.0).astype(BF16)
    member_l = lax.broadcasted_iota(jnp.int32, (members, cells), 0)
    member_r = lax.broadcasted_iota(jnp.int32, (members, cells), 1)
    same_member[...] = jnp.where(member_l == member_r // PIECE_ITEMS, 1.0, 0.0)

    def score(c):
        patches = [slice(p, p + PIECE_ITEMS) for p in range(0, ROWS, PIECE_ITEMS)]
        us = [forecast[:, at, :].reshape(cells, result) for at in patches]
        narrow = [u.astype(BF16) for u in us]
        by_item = jnp.concatenate(
            [
                jnp.sum((dot(u, u, last=True) * same_item[...]).reshape(members, PIECE_ITEMS, cells), axis=1)
                for u in narrow
            ],
            axis=0,
        )
        count = by_item.shape[0]
        grams = dot(jnp.concatenate(three_way(by_item), axis=0), ones[...])
        gram = (grams[:count] + grams[count : 2 * count] + grams[2 * count :]).reshape(
            len(patches), members, cells
        )
        mine = same_member[...][None]
        diagonal = gram * mine
        own_norm = jnp.sum(diagonal, axis=2, keepdims=True) * (1.0 / PIECE_ITEMS)
        other_norm = jnp.sum(diagonal, axis=1, keepdims=True)
        gap = (own_norm + other_norm - 2.0 * gram) * (1.0 - mine)
        weight = lax.rsqrt(gap + 1.0).astype(BF16).astype(F32)
        for p, at in enumerate(patches):
            u = us[p]
            spread_out = jnp.broadcast_to(weight[p][:, None, :], (members, PIECE_ITEMS, cells))
            mixing = spread_out.reshape(cells, cells) * same_item[...]
            total = jnp.sum(mixing, axis=1, keepdims=True)
            weighted = dot(mixing.astype(BF16), narrow[p])
            spread = (scale / members * (total * u - weighted)).astype(BF16)
            miss = (u.reshape(members, PIECE_ITEMS, result) - target[c, at, :][None]).reshape(u.shape)
            square = jnp.sum(miss * miss, axis=1, keepdims=True).reshape(members, PIECE_ITEMS, 1)
            norm = jnp.sqrt(jnp.sum(square, axis=1, keepdims=True) + 1.0)
            per_norm = jnp.broadcast_to(scale / norm, square.shape).reshape(cells, 1)
            cotangent[:, at, :] = (miss * per_norm - spread.astype(F32)).reshape(
                members, PIECE_ITEMS, result
            )

    for m in range(own):
        for k in far_first:
            first_piece(m, me, lax.rem(me + k, n)).wait_recv()

    groups = back_send.shape[0]

    @pl.loop(0, chunks)
    def _(c):
        g, part = c // 2, lax.rem(c, 2)

        @pl.when(c > 0)
        def _():
            for k in far_first:
                piece(c, me, lax.rem(me + k, n)).wait_recv()

        x = recv[c].reshape(members * ROWS, width)
        for h in range(0, hid, hid_tile):
            at = slice(h, h + hid_tile)
            gate = dot(x, wg_ref[:, at])
            up = dot(x, wu_ref[:, at])
            s = 0.5 * jnp.tanh(0.5 * gate) + 0.5
            gated = gate * s
            hidden[:, at] = (gated * up).astype(BF16)
            up_factor[:, at] = gated
            gate_factor[:, at] = up * (s + gated * (1.0 - s))
        value = dot(hidden[...], low_ref[...]).astype(BF16).astype(F32)
        forecast[...] = value.reshape(members, ROWS, result)
        score(c)
        ct = cotangent[...].reshape(members * ROWS, result).astype(BF16)
        for h in range(0, hid, hid_tile):
            at = slice(h, h + hid_tile)
            hidden_grad = dot(ct, low_t[:, at])
            for i, factor in enumerate((gate_factor, up_factor)):
                grad = (hidden_grad * factor[:, at]).astype(BF16).astype(F32)
                total = jnp.sum(grad.reshape(members, ROWS, hid_tile), axis=0)
                high = total.astype(BF16)
                grads[i, :ROWS, at] = high
                grads[i, ROWS:, at] = (total - high.astype(F32)).astype(BF16)
        y = dot(grads[0], wg_t[...]) + dot(grads[1], wu_t[...])
        y = y[:ROWS] + y[ROWS:]
        half = ROWS // 2
        for d in range(n):
            cols = slice(d * block, (d + 1) * block)
            parts = [y[:half, cols], y[half:, cols]]
            if 2 * block < LANES:
                parts.append(jnp.zeros((half, LANES - 2 * block), F32))
            pair[part, d] = jnp.concatenate(parts, axis=1)

        @pl.when((part == 1) | (c == chunks - 1))
        def _():
            back_send[g] = jnp.concatenate([pair[0], pair[1]], axis=1).astype(BF16)
            for k in far_first:
                back_piece(g, lax.rem(me + k, n), me).start()
            back_recv[me, g] = back_send[g, me]

    @pl.loop(0, groups)
    def _(g):
        for k in far_first:
            back_piece(g, me, lax.rem(me + k, n)).wait_recv()

    half = ROWS // 2
    packed = back_recv[...].reshape(n, groups * 2, half, LANES)[:, :chunks].astype(F32)
    low_half = packed.reshape(n * chunks, 1, half, LANES)
    high_half = pltpu.roll(packed.reshape(n * chunks * half, LANES), LANES - block, 1)
    patches = jnp.concatenate([low_half, high_half.reshape(low_half.shape)], axis=1)
    patches = patches.reshape(tokens, LANES).astype(BF16)
    out_ref[...] = dot(order_t[...], patches)[:, :block]

    for m in range(own):
        for k in far_first:
            first_piece(m, lax.rem(me + k, n), me).wait_send()

    @pl.loop(1, chunks)
    def _(c):
        for k in far_first:
            piece(c, lax.rem(me + k, n), me).wait_send()

    @pl.loop(0, groups)
    def _(g):
        for k in far_first:
            back_piece(g, lax.rem(me + k, n), me).wait_send()


def body(
    latents, sample_perturbation, noise_table, member_seed, piece_arrangement, targets,
    w_gate, w_up, lowering_matrix,
):
    n = lax.axis_size("member")
    own = sample_perturbation.shape[0]
    tokens, width = latents.shape
    hid, result = lowering_matrix.shape
    members = n * own
    chunks = tokens // (n * ROWS)
    block = width // n
    assert 2 * block <= LANES and chunks * n * ROWS == tokens == piece_arrangement.shape[0]
    vmem = pl.BlockSpec(memory_space=pltpu.VMEM)
    smem = pl.BlockSpec(memory_space=pltpu.SMEM)
    hbm = pl.BlockSpec(memory_space=pl.ANY)
    groups = (chunks + 1) // 2
    rows = members * ROWS
    return pl.pallas_call(
        functools.partial(kernel, n, own, chunks, block, 256),
        out_shape=jax.ShapeDtypeStruct((tokens, block), F32),
        in_specs=[smem] + [hbm] * 8,
        out_specs=vmem,
        scratch_shapes=[
            pltpu.VMEM(piece_arrangement.shape, jnp.int32),
            pltpu.VMEM(latents.shape, BF16),
            pltpu.VMEM(noise_table.shape, F32),
            pltpu.VMEM(sample_perturbation.shape, BF16),
            pltpu.VMEM(targets.shape, BF16),
            pltpu.VMEM(w_gate.shape, BF16),
            pltpu.VMEM(w_up.shape, BF16),
            pltpu.VMEM(lowering_matrix.shape, BF16),
            pltpu.VMEM((hid, width), BF16),
            pltpu.VMEM((hid, width), BF16),
            pltpu.VMEM((result, hid), BF16),
            pltpu.VMEM((n, chunks, ROWS, tokens), BF16),
            pltpu.VMEM((tokens, tokens), BF16),
            pltpu.VMEM((own, tokens, width), BF16),
            pltpu.VMEM((chunks, ROWS, result), F32),
            pltpu.VMEM((chunks, n, own, ROWS, width), BF16),
            pltpu.VMEM((chunks, members, ROWS, width), BF16),
            pltpu.VMEM((rows, hid), BF16),
            pltpu.VMEM((rows, hid), F32),
            pltpu.VMEM((rows, hid), F32),
            pltpu.VMEM((members, ROWS, result), F32),
            pltpu.VMEM((members, ROWS, result), F32),
            pltpu.VMEM((2, 2 * ROWS, hid), BF16),
            pltpu.VMEM((members * PIECE_ITEMS, members * PIECE_ITEMS), F32),
            pltpu.VMEM((members * PIECE_ITEMS, members * PIECE_ITEMS), BF16),
            pltpu.VMEM((members, members * PIECE_ITEMS), F32),
            pltpu.VMEM((2, n, ROWS // 2, LANES), F32),
            pltpu.VMEM((groups, n, ROWS, LANES), BF16),
            pltpu.VMEM((n, groups, ROWS, LANES), BF16),
            pltpu.SemaphoreType.DMA((7 + own,)),
            pltpu.SemaphoreType.DMA((chunks, n)),
            pltpu.SemaphoreType.DMA((chunks, n)),
            pltpu.SemaphoreType.DMA((own, n)),
            pltpu.SemaphoreType.DMA((own, n)),
            pltpu.SemaphoreType.DMA((groups, n)),
            pltpu.SemaphoreType.DMA((n, groups)),
        ],
        compiler_params=pltpu.CompilerParams(
            collective_id=0, has_side_effects=True, vmem_limit_bytes=64 * 1024 * 1024
        ),
        name="energy_score_gradient",
    )(
        member_seed, piece_arrangement, latents, noise_table, sample_perturbation,
        targets, w_gate, w_up, lowering_matrix,
    )


def solution(mesh):
    in_specs = (
        P("space", None),
        P("member", "space", None),
        P(),
        P("member"),
        P(),
        P("space", None),
        P(),
        P(),
        P(),
    )
    out_specs = P("space", "member")
    return jax.shard_map(body, mesh=mesh, in_specs=in_specs, out_specs=out_specs, check_vma=False)
```

```python
import functools

import jax
import jax.numpy as jnp
from jax import lax
from jax.experimental import pallas as pl
from jax.experimental.pallas import tpu as pltpu
from jax.sharding import PartitionSpec as P

PIECE_ITEMS = 8
ROWS = 16
LANES = 128
F32 = jnp.float32
BF16 = jnp.bfloat16


def dot(a, b, last=False):
    dims = (((1,), (1,)), ((), ())) if last else (((1,), (0,)), ((), ()))
    return lax.dot_general(a, b, dims, preferred_element_type=F32)


def three_way(x):
    high = x.astype(BF16)
    rest = x - high.astype(F32)
    mid = rest.astype(BF16)
    return high, mid, (rest - mid.astype(F32)).astype(BF16)


def kernel(
    n, own, chunks, block, hid_tile,
    seed_ref, arr_hbm, lat_hbm, table_hbm, pert_hbm, tgt_hbm, wg_hbm, wu_hbm, low_hbm,
    out_ref,
    arr_ref, lat_ref, table_ref, pert_ref, tgt_ref, wg_ref, wu_ref, low_ref,
    wg_t, wu_t, low_t,
    order, order_t, noisy, target, send, recv, hidden, gate_factor, up_factor, forecast, cotangent,
    grads, same_item, ones, same_member, back_send, back_recv,
    load_sem, send_sem, recv_sem, first_send_sem, first_recv_sem, back_send_sem, back_recv_sem,
):
    me = lax.axis_index("member")
    tokens, width = lat_ref.shape
    members = n * own
    hid = wg_ref.shape[1]
    result = low_ref.shape[1]
    scale = float(PIECE_ITEMS * result) ** 0.5
    side = n // 2
    mine_at, base = lax.rem(me, side), me // side * side
    other = side - base
    near = [base + lax.rem(mine_at + j, side) for j in range(1, side)]
    far = [other + lax.rem(mine_at + j, side) for j in range(side)]

    barrier = pltpu.get_barrier_semaphore()
    for k in range(1, n):
        pl.semaphore_signal(
            barrier, inc=1, device_id={"member": lax.rem(me + k, n)},
            device_id_type=pl.DeviceIdType.MESH,
        )
    loads = [
        pltpu.make_async_copy(src, dst, load_sem.at[i])
        for i, (src, dst) in enumerate(
            [(arr_hbm, arr_ref), (lat_hbm, lat_ref), (table_hbm, table_ref)]
            + [(pert_hbm.at[m], pert_ref.at[m]) for m in range(own)]
            + [(tgt_hbm, tgt_ref), (wg_hbm, wg_ref), (wu_hbm, wu_ref), (low_hbm, low_ref)]
        )
    ]
    for load in loads:
        load.start()

    def piece(c, d, s):
        return pltpu.make_async_remote_copy(
            src_ref=send.at[c, d],
            dst_ref=recv.at[c, pl.ds(s * own, own)],
            send_sem=send_sem.at[c, d],
            recv_sem=recv_sem.at[c, s],
            device_id={"member": d},
            device_id_type=pl.DeviceIdType.MESH,
        )

    def first_piece(m, d, s):
        return pltpu.make_async_remote_copy(
            src_ref=send.at[0, d, m],
            dst_ref=recv.at[0, s * own + m],
            send_sem=first_send_sem.at[m, d],
            recv_sem=first_recv_sem.at[m, s],
            device_id={"member": d},
            device_id_type=pl.DeviceIdType.MESH,
        )

    def back_piece(c, d, s):
        return pltpu.make_async_remote_copy(
            src_ref=back_send.at[c, d],
            dst_ref=back_recv.at[s, c],
            send_sem=back_send_sem.at[c, d],
            recv_sem=back_recv_sem.at[s, c],
            device_id={"member": d},
            device_id_type=pl.DeviceIdType.MESH,
        )

    loads[0].wait()
    arr_row = arr_ref[...].reshape(1, tokens)
    arr_col = jnp.transpose(jnp.broadcast_to(arr_row, (8, tokens)))[:, :1]
    def pick(c):
        token = lax.broadcasted_iota(jnp.int32, (n, ROWS, tokens), 2)
        place = arr_col.reshape(n, chunks, ROWS, 1)[:, c]
        order[:, c] = jnp.where(place == token, 1.0, 0.0).astype(BF16)

    pick(0)
    loads[1].wait()
    loads[2].wait()
    row_of = lax.broadcasted_iota(jnp.int32, table_ref.shape, 0)
    rows = order[:, 0].reshape(n * ROWS, tokens)
    for m in range(own):
        noise = jnp.sum(jnp.where(row_of == seed_ref[m], table_ref[...], 0.0), axis=0, keepdims=True)
        loads[3 + m].wait()
        noisy[m] = (lat_ref[...].astype(F32) + pert_ref[m].astype(F32) * noise).astype(BF16)
        send[0, :, m] = dot(rows, noisy[m]).astype(BF16).reshape(n, ROWS, width)
        if m == 0:
            pl.semaphore_wait(barrier, n - 1)
        for d in far + near:
            first_piece(m, d, me).start()
    recv[0, pl.ds(me * own, own)] = send[0, me]

    for c in range(1, chunks):
        pick(c)

    @pl.loop(1, chunks)
    def _(c):
        rows = order[:, c].reshape(n * ROWS, tokens)
        for m in range(own):
            send[c, :, m] = dot(rows, noisy[m]).astype(BF16).reshape(n, ROWS, width)
        for d in far + near:
            piece(c, d, me).start()
        recv[c, pl.ds(me * own, own)] = send[c, me]

    token = lax.broadcasted_iota(jnp.int32, (tokens, tokens), 0)
    order_t[...] = jnp.where(arr_row == token, 1.0, 0.0).astype(BF16)
    loads[3 + own].wait()
    target[...] = dot(order[me].reshape(chunks * ROWS, tokens), tgt_ref[...]).reshape(
        chunks, ROWS, result
    )
    for load in loads[4 + own :]:
        load.wait()
    wg_t[...] = jnp.transpose(wg_ref[...])
    wu_t[...] = jnp.transpose(wu_ref[...])
    low_t[...] = jnp.transpose(low_ref[...])

    cells = members * PIECE_ITEMS
    left = lax.broadcasted_iota(jnp.int32, (cells, cells), 0)
    right = lax.broadcasted_iota(jnp.int32, (cells, cells), 1)
    same_item[...] = jnp.where((left & (PIECE_ITEMS - 1)) == (right & (PIECE_ITEMS - 1)), 1.0, 0.0)
    ones[...] = jnp.where(left // PIECE_ITEMS == right // PIECE_ITEMS, 1.0, 0.0).astype(BF16)
    member_l = lax.broadcasted_iota(jnp.int32, (members, cells), 0)
    member_r = lax.broadcasted_iota(jnp.int32, (members, cells), 1)
    same_member[...] = jnp.where(member_l == member_r // PIECE_ITEMS, 1.0, 0.0)

    def score(c):
        patches = [slice(p, p + PIECE_ITEMS) for p in range(0, ROWS, PIECE_ITEMS)]
        us = [forecast[:, at, :].reshape(cells, result) for at in patches]
        narrow = [u.astype(BF16) for u in us]
        by_item = jnp.concatenate(
            [
                jnp.sum((dot(u, u, last=True) * same_item[...]).reshape(members, PIECE_ITEMS, cells), axis=1)
                for u in narrow
            ],
            axis=0,
        )
        count = by_item.shape[0]
        grams = dot(jnp.concatenate(three_way(by_item), axis=0), ones[...])
        gram = (grams[:count] + grams[count : 2 * count] + grams[2 * count :]).reshape(
            len(patches), members, cells
        )
        mine = same_member[...][None]
        diagonal = gram * mine
        own_norm = jnp.sum(diagonal, axis=2, keepdims=True) * (1.0 / PIECE_ITEMS)
        other_norm = jnp.sum(diagonal, axis=1, keepdims=True)
        gap = (own_norm + other_norm - 2.0 * gram) * (1.0 - mine)
        weight = lax.rsqrt(gap + 1.0).astype(BF16).astype(F32)
        for p, at in enumerate(patches):
            u = us[p]
            spread_out = jnp.broadcast_to(weight[p][:, None, :], (members, PIECE_ITEMS, cells))
            mixing = spread_out.reshape(cells, cells) * same_item[...]
            total = jnp.sum(mixing, axis=1, keepdims=True)
            weighted = dot(mixing.astype(BF16), narrow[p])
            spread = (scale / members * (total * u - weighted)).astype(BF16)
            miss = (u.reshape(members, PIECE_ITEMS, result) - target[c, at, :][None]).reshape(u.shape)
            square = jnp.sum(miss * miss, axis=1, keepdims=True).reshape(members, PIECE_ITEMS, 1)
            norm = jnp.sqrt(jnp.sum(square, axis=1, keepdims=True) + 1.0)
            per_norm = jnp.broadcast_to(scale / norm, square.shape).reshape(cells, 1)
            cotangent[:, at, :] = (miss * per_norm - spread.astype(F32)).reshape(
                members, PIECE_ITEMS, result
            )

    def arrive(c, sources):
        @pl.when(c == 0)
        def _():
            for m in range(own):
                for s in sources:
                    first_piece(m, me, s).wait_recv()

        @pl.when(c > 0)
        def _():
            for s in sources:
                piece(c, me, s).wait_recv()

    side_rows = side * own * ROWS

    def forward(c, start):
        x = recv[c, pl.ds(start * own, side * own)].reshape(side_rows, width)
        half_at = start // side
        for h in range(0, hid, hid_tile):
            at = slice(h, h + hid_tile)
            gate = dot(x, wg_ref[:, at])
            up = dot(x, wu_ref[:, at])
            s = 0.5 * jnp.tanh(0.5 * gate) + 0.5
            gated = gate * s
            hidden[half_at, :, at] = (gated * up).astype(BF16)
            up_factor[half_at, :, at] = gated
            gate_factor[half_at, :, at] = up * (s + gated * (1.0 - s))

    @pl.loop(0, chunks)
    def _(c):
        arrive(c, near)
        forward(c, base)
        arrive(c, far)
        forward(c, other)
        value = dot(hidden[...].reshape(members * ROWS, hid), low_ref[...]).astype(BF16).astype(F32)
        forecast[...] = value.reshape(members, ROWS, result)
        score(c)
        ct = cotangent[...].reshape(members * ROWS, result).astype(BF16)
        for h in range(0, hid, hid_tile):
            at = slice(h, h + hid_tile)
            hidden_grad = dot(ct, low_t[:, at])
            for i, factor in enumerate((gate_factor, up_factor)):
                grad = (hidden_grad * factor[:, :, at].reshape(hidden_grad.shape)).astype(BF16).astype(F32)
                total = jnp.sum(grad.reshape(members, ROWS, hid_tile), axis=0)
                high = total.astype(BF16)
                grads[i, :ROWS, at] = high
                grads[i, ROWS:, at] = (total - high.astype(F32)).astype(BF16)
        y = dot(grads[0], wg_t[...]) + dot(grads[1], wu_t[...])
        y = y[:ROWS] + y[ROWS:]
        half = ROWS // 2
        for d in range(n):
            cols = slice(d * block, (d + 1) * block)
            parts = [y[:half, cols], y[half:, cols]]
            if 2 * block < LANES:
                parts.append(jnp.zeros((half, LANES - 2 * block), F32))
            back_send[c, d] = jnp.concatenate(parts, axis=1)
        for d in far + near:
            back_piece(c, d, me).start()
        back_recv[me, c] = back_send[c, me]

    @pl.loop(0, chunks)
    def _(c):
        for s in near + far:
            back_piece(c, me, s).wait_recv()

    half = ROWS // 2
    packed = back_recv[...].reshape(n * chunks * half, LANES)
    low_half = packed.reshape(n * chunks, 1, half, LANES)
    high_half = pltpu.roll(packed, LANES - block, 1).reshape(low_half.shape)
    patches = jnp.concatenate([low_half, high_half], axis=1).reshape(tokens, LANES)
    placed = dot(order_t[...], jnp.concatenate(three_way(patches), axis=1))
    placed = placed[:, :LANES] + placed[:, LANES : 2 * LANES] + placed[:, 2 * LANES :]
    out_ref[...] = placed[:, :block]

    for m in range(own):
        for d in far + near:
            first_piece(m, d, me).wait_send()

    @pl.loop(1, chunks)
    def _(c):
        for d in far + near:
            piece(c, d, me).wait_send()

    @pl.loop(0, chunks)
    def _(c):
        for d in far + near:
            back_piece(c, d, me).wait_send()


def body(
    latents, sample_perturbation, noise_table, member_seed, piece_arrangement, targets,
    w_gate, w_up, lowering_matrix,
):
    n = lax.axis_size("member")
    own = sample_perturbation.shape[0]
    tokens, width = latents.shape
    hid, result = lowering_matrix.shape
    members = n * own
    chunks = tokens // (n * ROWS)
    block = width // n
    assert 2 * block <= LANES and chunks * n * ROWS == tokens == piece_arrangement.shape[0]
    vmem = pl.BlockSpec(memory_space=pltpu.VMEM)
    smem = pl.BlockSpec(memory_space=pltpu.SMEM)
    hbm = pl.BlockSpec(memory_space=pl.ANY)
    rows = members * ROWS
    return pl.pallas_call(
        functools.partial(kernel, n, own, chunks, block, 256),
        out_shape=jax.ShapeDtypeStruct((tokens, block), F32),
        in_specs=[smem] + [hbm] * 8,
        out_specs=vmem,
        scratch_shapes=[
            pltpu.VMEM(piece_arrangement.shape, jnp.int32),
            pltpu.VMEM(latents.shape, BF16),
            pltpu.VMEM(noise_table.shape, F32),
            pltpu.VMEM(sample_perturbation.shape, BF16),
            pltpu.VMEM(targets.shape, BF16),
            pltpu.VMEM(w_gate.shape, BF16),
            pltpu.VMEM(w_up.shape, BF16),
            pltpu.VMEM(lowering_matrix.shape, BF16),
            pltpu.VMEM((hid, width), BF16),
            pltpu.VMEM((hid, width), BF16),
            pltpu.VMEM((result, hid), BF16),
            pltpu.VMEM((n, chunks, ROWS, tokens), BF16),
            pltpu.VMEM((tokens, tokens), BF16),
            pltpu.VMEM((own, tokens, width), BF16),
            pltpu.VMEM((chunks, ROWS, result), F32),
            pltpu.VMEM((chunks, n, own, ROWS, width), BF16),
            pltpu.VMEM((chunks, members, ROWS, width), BF16),
            pltpu.VMEM((2, rows // 2, hid), BF16),
            pltpu.VMEM((2, rows // 2, hid), F32),
            pltpu.VMEM((2, rows // 2, hid), F32),
            pltpu.VMEM((members, ROWS, result), F32),
            pltpu.VMEM((members, ROWS, result), F32),
            pltpu.VMEM((2, 2 * ROWS, hid), BF16),
            pltpu.VMEM((members * PIECE_ITEMS, members * PIECE_ITEMS), F32),
            pltpu.VMEM((members * PIECE_ITEMS, members * PIECE_ITEMS), BF16),
            pltpu.VMEM((members, members * PIECE_ITEMS), F32),
            pltpu.VMEM((chunks, n, ROWS // 2, LANES), F32),
            pltpu.VMEM((n, chunks, ROWS // 2, LANES), F32),
            pltpu.SemaphoreType.DMA((7 + own,)),
            pltpu.SemaphoreType.DMA((chunks, n)),
            pltpu.SemaphoreType.DMA((chunks, n)),
            pltpu.SemaphoreType.DMA((own, n)),
            pltpu.SemaphoreType.DMA((own, n)),
            pltpu.SemaphoreType.DMA((chunks, n)),
            pltpu.SemaphoreType.DMA((n, chunks)),
        ],
        compiler_params=pltpu.CompilerParams(
            collective_id=0, has_side_effects=True, vmem_limit_bytes=64 * 1024 * 1024
        ),
        name="energy_score_gradient",
    )(
        member_seed, piece_arrangement, latents, noise_table, sample_perturbation,
        targets, w_gate, w_up, lowering_matrix,
    )


def solution(mesh):
    in_specs = (
        P("space", None),
        P("member", "space", None),
        P(),
        P("member"),
        P(),
        P("space", None),
        P(),
        P(),
        P(),
    )
    out_specs = P("space", "member")
    return jax.shard_map(body, mesh=mesh, in_specs=in_specs, out_specs=out_specs, check_vma=False)
```
